32 devices in a mesh: groups: 2 (over x), stem: 8 (over z, y), cuts: 2 (over core).
Axes of the slice: x: 2, y: 2, z: 4, core: 2. Of those that a mesh axis runs over, the one named last changes fastest.
Arguments:
- stem: bfloat16 [4, 2, 4096, 1024], P(('groups', 'cuts'), None, 'stem'), parts along dimension 0, may hold values from -6 to 6
- edge_values: int32 [4, 4], P(('groups', 'cuts')), parts along dimension 0, may hold values from 0 to 1
- index_order: int32 [1024], replicated, may hold values from 0 to 1023, each once
- branch_first: bfloat16 [2, 1024, 1024], replicated, may hold values from -0.125 to 0.125
- branch_second: bfloat16 [2, 1024, 1024], replicated, may hold values from -0.125 to 0.125
- branch_third: bfloat16 [2, 1024, 256], replicated, may hold values from -0.125 to 0.125
- edge_table: float32 [16, 2, 256], replicated, may hold values from -6 to 6
- picks: int32 [4096], P('stem'), may hold values from 0 to 511, as said below
Outputs:
- amplitudes: float32 [2, 8192, 256], P(None, ('groups', 'stem')), parts along dimension 1
The draws below stay inside these ranges and needn't reach their ends.
There are 2 independent parts, one for each index of `groups`. The reference program is written for one: setup_inputs(seed, part) draws one part's arguments, and reference() takes and returns one part's arrays. A program takes and returns all parts, laid end to end along the dimension named above; an argument that names none is the same for every part. Nothing has to cross between parts.
Inputs may be any that keep to these rules, and one draw needn't show every extreme that they name: `index_order`: each number of 0 to 1023 once. `picks`: each aligned block of 512 entries names every number of 0 to 511 once.
All inputs are finite; a program needn't handle non-finite values.
Results may differ from the reference program's by a relative error of at most 0.0041.
Values may be sent and summed in bfloat16 or wider, within the bound.
A program may use at most 64 MiB of HBM per device.

```python
import jax
import jax.numpy as jnp

K = 1024
KC = 256
ROWS_DEV = 512
PICKS = 512
EDGES = 4
CODES = 16
SLICES = 2
ROWS = 4096
OUT_ROWS = 4096
N_STEM = 8


def draw_picks(key, part):
    block_keys = jax.random.split(key, OUT_ROWS // ROWS_DEV)
    blocks = jax.vmap(lambda block_key: jax.random.permutation(block_key, ROWS_DEV))(block_keys)
    return blocks.reshape(-1).astype(jnp.int32)


def set_ends(drawn, rng, smallest, top_value):
    index_at = [jax.random.randint(jax.random.fold_in(rng, axis), (), 0, length) for axis, length in enumerate(drawn.shape)]
    longest = drawn.shape.index(max(drawn.shape))
    next_to = index_at[:longest] + [(index_at[longest] + 1) % drawn.shape[longest]] + index_at[longest + 1:]
    return drawn.at[tuple(index_at)].set(smallest).at[tuple(next_to)].set(top_value)


def level_of(key, shape, shards, low, high):
    def one(axis_at, shards_of):
        draws = jax.random.uniform(jax.random.fold_in(jax.random.fold_in(key, 6), axis_at), (shards_of,), jnp.float32, low / len(shards), high / len(shards))
        return jnp.repeat(jnp.exp(draws), shape[axis_at] // shards_of).reshape((-1,) + (1,) * (len(shape) - axis_at - 1))

    level = one(*shards[0])
    for cut in shards[1:]:
        level = level * one(*cut)
    return level


def scatter_about(own_key, extent, spread, limit, shards=(), held_as=jnp.bfloat16):
    array = jax.random.normal(own_key, extent, jnp.float32) * spread
    if len(shards) > 0:
        array = level_of(own_key, extent, shards, -0.22, 0.18) * array
    return jnp.clip(array, min=-limit, max=limit).astype(held_as)


def setup_inputs(seed: int = 0, part: int = 0) -> dict:
    splits = jax.random.split(jax.random.key(seed), 9)
    own_keys = jax.random.split(jax.random.fold_in(splits[8], part), 9)
    stem = scatter_about(own_keys[0], (SLICES, 2, ROWS, K), 1.0, 6.0, ((0, 2), (2, 8)))
    edge_values = set_ends(jax.random.randint(own_keys[1], (SLICES, EDGES), 0, 2), jax.random.fold_in(own_keys[1], 1), 0, 1).astype(jnp.int32)
    index_order = jax.random.permutation(splits[2], K).astype(jnp.int32)
    branch_first = scatter_about(splits[3], (2, K, K), (2 * K) ** -0.5, 0.125)
    branch_second = scatter_about(splits[4], (2, K, K), (2 * K) ** -0.5, 0.125)
    branch_third = scatter_about(splits[5], (2, K, KC), (2 * K) ** -0.5, 0.125)
    edge_table = scatter_about(splits[6], (CODES, 2, KC), 1.0, 6.0, (), jnp.float32)
    picks = draw_picks(jax.random.fold_in(splits[8], 71), part)
    return {"stem": stem, "edge_values": edge_values, "index_order": index_order, "branch_first": branch_first, "branch_second": branch_second, "branch_third": branch_third, "edge_table": edge_table, "picks": picks}


def complex_dot(operand, matrix):
    real = jnp.dot(operand[0], matrix[0], preferred_element_type=jnp.float32) - jnp.dot(operand[1], matrix[1], preferred_element_type=jnp.float32)
    imag = jnp.dot(operand[0], matrix[1], preferred_element_type=jnp.float32) + jnp.dot(operand[1], matrix[0], preferred_element_type=jnp.float32)
    return jnp.stack([real, imag])


def reference(stem, edge_values, index_order, branch_first, branch_second, branch_third, edge_table, picks):
    half_axis = N_STEM // 2
    block_rows = ROWS_DEV // N_STEM
    row_ids = (jnp.arange(N_STEM * PICKS, dtype=jnp.int32) // PICKS) * ROWS_DEV + picks
    powers = 2 ** jnp.arange(EDGES, dtype=jnp.int32)
    total = jnp.zeros((2, N_STEM * PICKS, KC), jnp.float32)
    for slice_id in range(SLICES):
        first = complex_dot(stem[slice_id], branch_first).astype(jnp.bfloat16)
        viewed = first.reshape(2, 2, half_axis, ROWS_DEV, 2, K // 2)
        swapped = jnp.transpose(viewed, (0, 4, 2, 3, 1, 5)).reshape(2, N_STEM * ROWS_DEV, K)
        permuted = jnp.take(swapped, index_order, axis=2)
        second = complex_dot(permuted, branch_second).astype(jnp.bfloat16)
        moved = jnp.swapaxes(second.reshape(2, N_STEM, N_STEM, block_rows, K), 1, 2).reshape(2, N_STEM * ROWS_DEV, K)
        picked = jnp.take(moved, row_ids, axis=1)
        third = complex_dot(picked, branch_third)
        code = jnp.sum(edge_values[slice_id] * powers)
        factor = edge_table[code]
        real = third[0] * factor[0][None, :] - third[1] * factor[1][None, :]
        imag = third[0] * factor[1][None, :] + third[1] * factor[0][None, :]
        total = total + jnp.stack([real, imag])
    return total
```

```python
import functools

import jax
import jax.numpy as jnp
from jax import lax
from jax.experimental import pallas as pl
from jax.experimental.pallas import tpu as pltpu
from jax.sharding import PartitionSpec as P

MESH = pl.DeviceIdType.MESH
CHUNKS = 4


def dot(a, b):
    return jnp.dot(a, b, preferred_element_type=jnp.float32)


def contract_kernel(
    n, edges_ref, order_ref, table_ref, stem_hbm, first_hbm, second_hbm, third_hbm, out_hbm,
    stem, b1, b2, b3, pick, joint, gathered, firsts, partial, other, slab,
    load_sem, own_sem, pass_send, pass_recv, send_sem, recv_sem, copy_send, copy_recv,
):
    me = lax.axis_index("stem")
    core = lax.axis_index("cuts")
    mate = 1 - core
    half = n // 2
    top = me // half
    _, rows, width = stem.shape
    open_width = table_ref.shape[2]
    part = open_width // 2
    half_width = width // 2
    chunk = rows // CHUNKS
    block = rows // n
    owners = chunk // block

    loads = [
        pltpu.make_async_copy(second_hbm.at[0], b2.at[0], load_sem.at[0]),
        pltpu.make_async_copy(second_hbm.at[1], b2.at[1], load_sem.at[1]),
        pltpu.make_async_copy(third_hbm.at[0], b3.at[:, pl.ds(0, open_width)], load_sem.at[2]),
        pltpu.make_async_copy(third_hbm.at[1], b3.at[:, pl.ds(open_width, open_width)], load_sem.at[3]),
        pltpu.make_async_copy(first_hbm, b1, load_sem.at[4]),
        pltpu.make_async_copy(stem_hbm, stem, load_sem.at[5]),
    ]
    for load in loads:
        load.start()

    barrier = pltpu.get_barrier_semaphore()
    pl.semaphore_signal(barrier, inc=1, device_id={"cuts": mate}, device_id_type=MESH)

    @pl.loop(1, n)
    def _(step):
        pl.semaphore_signal(barrier, inc=1, device_id={"stem": (me + step) % n}, device_id_type=MESH)

    code = edges_ref[0, 0]
    for edge in range(1, edges_ref.shape[1]):
        code = code + edges_ref[0, edge] * 2**edge
    factor = table_ref[code]
    factor_re, factor_im = factor[0:1], factor[1:2]

    tile = half_width // 4
    for at in range(4):
        wanted = lax.broadcasted_iota(jnp.int32, (tile, width), 0) + (top * half_width + at * tile)
        hit = (order_ref[...] == wanted).astype(jnp.float32).astype(jnp.bfloat16)
        pick[at * tile : (at + 1) * tile, :] = hit

    for load in loads[:4]:
        load.wait()
    tall = width // 4

    @pl.loop(0, 4)
    def _(at):
        here = pl.ds(pl.multiple_of(at * tall, tall), tall)
        by_re = dot(b2[0, here, :], b3[...])
        by_im = dot(b2[1, here, :], b3[...])
        real = by_re[:, :open_width] - by_im[:, open_width:]
        imag = by_re[:, open_width:] + by_im[:, :open_width]
        joint[here, :open_width] = (real * factor_re - imag * factor_im).astype(jnp.bfloat16)
        joint[here, open_width:] = (real * factor_im + imag * factor_re).astype(jnp.bfloat16)

    gathered[...] = dot(pick[...], joint[...]).astype(jnp.bfloat16)

    for load in loads[4:]:
        load.wait()
    pl.semaphore_wait(barrier, n)

    def start_of(index):
        return (index + (1 - top) * (CHUNKS // 2)) % CHUNKS

    def passing(index):
        return pltpu.make_async_remote_copy(
            src_ref=partial.at[index, :, :, pl.ds(pl.multiple_of(mate * part, part), part)],
            dst_ref=other.at[index],
            send_sem=pass_send.at[index],
            recv_sem=pass_recv.at[index],
            device_id={"cuts": mate},
            device_id_type=MESH,
        )

    def sending(owner):
        return pltpu.make_async_remote_copy(
            src_ref=slab.at[owner],
            dst_ref=out_hbm.at[core, me],
            send_sem=send_sem.at[owner],
            recv_sem=recv_sem.at[me],
            device_id={"stem": owner},
            device_id_type=MESH,
        )

    def receiving(source):
        return pltpu.make_async_remote_copy(
            src_ref=slab.at[source],
            dst_ref=out_hbm.at[core, source],
            send_sem=send_sem.at[source],
            recv_sem=recv_sem.at[source],
            device_id={"stem": source},
            device_id_type=MESH,
        )

    def copying(source, src, column):
        return pltpu.make_async_remote_copy(
            src_ref=src,
            dst_ref=out_hbm.at[column, source],
            send_sem=copy_send.at[source],
            recv_sem=copy_recv.at[source],
            device_id={"cuts": mate},
            device_id_type=MESH,
        )

    @pl.loop(0, CHUNKS + 1)
    def _(index):
        @pl.when(index < CHUNKS)
        def _():
            here = pl.ds(pl.multiple_of(start_of(index) * chunk, chunk), chunk)
            step = open_width
            operand = stem[:, here, :].reshape(2 * chunk, width)
            for at in range(0, width, step):
                by_re = dot(operand, b1[0, :, at : at + step])
                by_im = dot(operand, b1[1, :, at : at + step])
                firsts[:chunk, at : at + step] = (by_re[:chunk] - by_im[chunk:]).astype(jnp.bfloat16)
                firsts[chunk:, at : at + step] = (by_im[:chunk] + by_re[chunk:]).astype(jnp.bfloat16)
            for t in range(2):
                got = dot(firsts[:, t * half_width : (t + 1) * half_width], gathered[...])
                partial[index, t] = got[:chunk, :open_width] - got[chunk:, open_width:]
                partial[index, 2 + t] = got[:chunk, open_width:] + got[chunk:, :open_width]
            passing(index).start()

        @pl.when(index > 0)
        def _():
            last = index - 1
            passing(last).wait_recv()
            mine = pl.ds(pl.multiple_of(core * part, part), part)
            total = partial[last, :, :, mine] + other[last]
            for at in range(owners):
                owner = start_of(last) * owners + at
                for c in range(2):
                    both = [total[2 * c + t, at * block : (at + 1) * block] for t in range(2)]
                    slab[owner, c] = jnp.concatenate(both, axis=0).astype(jnp.bfloat16)

                @pl.when(owner != me)
                def _():
                    sending(owner).start()

    own = pltpu.make_async_copy(slab.at[me], out_hbm.at[core, me], own_sem)
    own.start()
    copying(me, slab.at[me], core).start()

    @pl.loop(1, n)
    def _(step):
        source = (me + step) % half + ((top + step // half) % 2) * half
        receiving(source).wait_recv()
        copying(source, out_hbm.at[core, source], core).start()

    own.wait()

    @pl.loop(0, n)
    def _(source):
        copying(source, out_hbm.at[core, source], mate).wait()

        @pl.when(source != me)
        def _():
            receiving(source).wait_send()

    @pl.loop(0, CHUNKS)
    def _(index):
        passing(index).wait_send()


def pick_kernel(n, picks_ref, parts_ref, out_ref):
    half = n // 2
    rows = out_ref.shape[1]
    block = rows // n
    part = parts_ref.shape[4]
    at = lax.broadcasted_iota(jnp.int32, (rows, rows), 0)
    u, rest = at // (2 * block), at % (2 * block)
    row = (rest // block) * (half * block) + u * block + rest % block
    hit = (picks_ref[...] == row).astype(jnp.float32).astype(jnp.bfloat16)
    for c in range(2):
        total = None
        for h in range(2):
            sides = [parts_ref[k, h * half : (h + 1) * half, c].reshape(rows, part) for k in range(2)]
            got = lax.dot_general(
                hit, jnp.concatenate(sides, axis=1), (((0,), (0,)), ((), ())), preferred_element_type=jnp.float32
            )
            total = got if total is None else total + got
        out_ref[c] = total


def solution(mesh):
    n = mesh.shape["stem"]

    def on_device(stem, edge_values, index_order, branch_first, branch_second, branch_third, edge_table, picks):
        _, _, rows, width = stem.shape
        open_width = branch_third.shape[2]
        part = open_width // 2
        block = rows // n
        chunk = rows // CHUNKS
        bf16, f32 = jnp.bfloat16, jnp.float32
        vmem = pl.BlockSpec(memory_space=pltpu.VMEM)
        anywhere = pl.BlockSpec(memory_space=pl.ANY)
        dma = pltpu.SemaphoreType.DMA
        parts = pl.pallas_call(
            functools.partial(contract_kernel, n),
            out_shape=jax.ShapeDtypeStruct((2, n, 2, 2 * block, part), bf16),
            in_specs=[pl.BlockSpec(memory_space=pltpu.SMEM), vmem, vmem] + [anywhere] * 4,
            out_specs=anywhere,
            scratch_shapes=[
                pltpu.VMEM((2, rows, width), bf16),
                pltpu.VMEM((2, width, width), bf16),
                pltpu.VMEM((2, width, width), bf16),
                pltpu.VMEM((width, 2 * open_width), bf16),
                pltpu.VMEM((width // 2, width), bf16),
                pltpu.VMEM((width, 2 * open_width), bf16),
                pltpu.VMEM((width // 2, 2 * open_width), bf16),
                pltpu.VMEM((2 * chunk, width), bf16),
                pltpu.VMEM((CHUNKS, 4, chunk, open_width), f32),
                pltpu.VMEM((CHUNKS, 4, chunk, part), f32),
                pltpu.VMEM((n, 2, 2 * block, part), bf16),
                dma((6,)),
                dma,
                dma((CHUNKS,)),
                dma((CHUNKS,)),
                dma((n,)),
                dma((n,)),
                dma((n,)),
                dma((n,)),
            ],
            compiler_params=pltpu.CompilerParams(
                collective_id=0, has_side_effects=True, vmem_limit_bytes=48 * 2**20
            ),
            cost_estimate=pl.CostEstimate(flops=8 * 10**9, bytes_accessed=13 * 2**20, transcendentals=0),
        )(
            edge_values, index_order.reshape(1, width), edge_table,
            stem[0], branch_first, branch_second, branch_third,
        )
        return pl.pallas_call(
            functools.partial(pick_kernel, n),
            out_shape=jax.ShapeDtypeStruct((2, picks.shape[0], open_width), f32),
            in_specs=[vmem, vmem],
            out_specs=vmem,
            compiler_params=pltpu.CompilerParams(vmem_limit_bytes=32 * 2**20),
        )(picks.reshape(1, picks.shape[0]), parts)

    return jax.shard_map(
        on_device,
        mesh=mesh,
        in_specs=(
            P(("groups", "cuts"), None, "stem", None),
            P(("groups", "cuts"), None),
            P(),
            P(),
            P(),
            P(),
            P(),
            P("stem"),
        ),
        out_specs=P(None, ("groups", "stem"), None),
        check_vma=False,
    )
```

```python
import functools

import jax
import jax.numpy as jnp
from jax import lax
from jax.experimental import pallas as pl
from jax.experimental.pallas import tpu as pltpu
from jax.sharding import PartitionSpec as P

MESH = pl.DeviceIdType.MESH
CHUNKS = 8
TILES = 4


def dot(a, b):
    return jnp.dot(a, b, preferred_element_type=jnp.float32)


def contract_kernel(
    n, edges_hbm, order_hbm, table_hbm, stem_hbm, first_hbm, second_hbm, third_hbm, out_hbm,
    edges_ref, order_ref, table_ref, stem, b1, b2, b3, pick, joint, gathered, firsts, partial, other, slab,
    load_sem, tile_sem, own_sem, pass_send, pass_recv, send_sem, recv_sem, copy_send, copy_recv,
):
    me = lax.axis_index("stem")
    core = lax.axis_index("cuts")
    mate = 1 - core
    half = n // 2
    top = me // half
    _, rows, width = stem.shape
    open_width = table_ref.shape[2]
    part = open_width // 2
    half_width = width // 2
    chunk = rows // CHUNKS
    block = rows // n
    owners = chunk // block

    tall = width // TILES
    loads = [
        pltpu.make_async_copy(third_hbm.at[0], b3.at[:, pl.ds(0, open_width)], load_sem.at[0]),
        pltpu.make_async_copy(third_hbm.at[1], b3.at[:, pl.ds(open_width, open_width)], load_sem.at[1]),
        pltpu.make_async_copy(order_hbm, order_ref, load_sem.at[2]),
        pltpu.make_async_copy(table_hbm, table_ref, load_sem.at[3]),
        pltpu.make_async_copy(edges_hbm, edges_ref, load_sem.at[4]),
    ]
    tiles = [
        pltpu.make_async_copy(
            second_hbm.at[:, pl.ds(at * tall, tall)], b2.at[:, pl.ds(at * tall, tall)], tile_sem.at[at]
        )
        for at in range(TILES)
    ]
    later = [
        pltpu.make_async_copy(stem_hbm, stem, load_sem.at[5]),
        pltpu.make_async_copy(first_hbm, b1, load_sem.at[6]),
    ]
    for load in loads + tiles:
        load.start()

    barrier = pltpu.get_barrier_semaphore()
    pl.semaphore_signal(barrier, inc=1, device_id={"cuts": mate}, device_id_type=MESH)

    @pl.loop(1, n)
    def _(step):
        pl.semaphore_signal(barrier, inc=1, device_id={"stem": (me + step) % n}, device_id_type=MESH)

    for load in loads:
        load.wait()
    wide = half_width // TILES
    for at in range(TILES):
        wanted = lax.broadcasted_iota(jnp.int32, (wide, width), 0) + (top * half_width + at * wide)
        hit = (order_ref[...] == wanted).astype(jnp.float32).astype(jnp.bfloat16)
        pick[at * wide : (at + 1) * wide, :] = hit

    code = edges_ref[0, 0]
    for edge in range(1, edges_ref.shape[1]):
        code = code + edges_ref[0, edge] * 2**edge
    factor = table_ref[code]
    factor_re, factor_im = factor[0:1], factor[1:2]

    for at in range(TILES):
        tiles[at].wait()
        if at == 0:
            for load in later:
                load.start()
        here = slice(at * tall, (at + 1) * tall)
        by_re = dot(b2[0, here, :], b3[...])
        by_im = dot(b2[1, here, :], b3[...])
        real = by_re[:, :open_width] - by_im[:, open_width:]
        imag = by_re[:, open_width:] + by_im[:, :open_width]
        joint[here, :open_width] = (real * factor_re - imag * factor_im).astype(jnp.bfloat16)
        joint[here, open_width:] = (real * factor_im + imag * factor_re).astype(jnp.bfloat16)

    gathered[...] = dot(pick[...], joint[...]).astype(jnp.bfloat16)

    for load in later:
        load.wait()

    def start_of(index):
        return (index + (1 - top) * (CHUNKS // 2)) % CHUNKS

    def passing(index):
        return pltpu.make_async_remote_copy(
            src_ref=partial.at[index, :, :, pl.ds(pl.multiple_of(mate * part, part), part)],
            dst_ref=other.at[index],
            send_sem=pass_send.at[index],
            recv_sem=pass_recv.at[index],
            device_id={"cuts": mate},
            device_id_type=MESH,
        )

    def sending(owner):
        return pltpu.make_async_remote_copy(
            src_ref=slab.at[owner],
            dst_ref=out_hbm.at[core, me],
            send_sem=send_sem.at[owner],
            recv_sem=recv_sem.at[me],
            device_id={"stem": owner},
            device_id_type=MESH,
        )

    def receiving(source):
        return pltpu.make_async_remote_copy(
            src_ref=slab.at[source],
            dst_ref=out_hbm.at[core, source],
            send_sem=send_sem.at[source],
            recv_sem=recv_sem.at[source],
            device_id={"stem": source},
            device_id_type=MESH,
        )

    def copying(source, src, column):
        return pltpu.make_async_remote_copy(
            src_ref=src,
            dst_ref=out_hbm.at[column, source],
            send_sem=copy_send.at[source],
            recv_sem=copy_recv.at[source],
            device_id={"cuts": mate},
            device_id_type=MESH,
        )

    def compute(index):
        here = pl.ds(pl.multiple_of(start_of(index) * chunk, chunk), chunk)
        step = open_width
        operand = stem[:, here, :].reshape(2 * chunk, width)
        for at in range(0, width, step):
            by_re = dot(operand, b1[0, :, at : at + step])
            by_im = dot(operand, b1[1, :, at : at + step])
            firsts[:chunk, at : at + step] = (by_re[:chunk] - by_im[chunk:]).astype(jnp.bfloat16)
            firsts[chunk:, at : at + step] = (by_im[:chunk] + by_re[chunk:]).astype(jnp.bfloat16)
        for t in range(2):
            got = dot(firsts[:, t * half_width : (t + 1) * half_width], gathered[...])
            partial[index, t] = got[:chunk, :open_width] - got[chunk:, open_width:]
            partial[index, 2 + t] = got[:chunk, open_width:] + got[chunk:, :open_width]

    def finish(last):
        passing(last).wait_recv()
        mine = pl.ds(pl.multiple_of(core * part, part), part)
        total = partial[last, :, :, mine] + other[last]
        for at in range(owners):
            owner = start_of(last) * owners + at
            for c in range(2):
                both = [total[2 * c + t, at * block : (at + 1) * block] for t in range(2)]
                slab[owner, c] = jnp.concatenate(both, axis=0).astype(jnp.bfloat16)

            @pl.when(owner != me)
            def _():
                sending(owner).start()

    compute(0)
    pl.semaphore_wait(barrier, n)
    passing(0).start()

    @pl.loop(1, CHUNKS)
    def _(index):
        compute(index)
        passing(index).start()
        finish(index - 1)

    finish(CHUNKS - 1)

    own = pltpu.make_async_copy(slab.at[me], out_hbm.at[core, me], own_sem)
    own.start()
    copying(me, slab.at[me], core).start()

    @pl.loop(1, n)
    def _(step):
        source = (me + step) % half + ((top + step // half) % 2) * half
        receiving(source).wait_recv()
        copying(source, out_hbm.at[core, source], core).start()

    own.wait()

    @pl.loop(0, n)
    def _(source):
        copying(source, out_hbm.at[core, source], mate).wait()

        @pl.when(source != me)
        def _():
            receiving(source).wait_send()

    @pl.loop(0, CHUNKS)
    def _(index):
        passing(index).wait_send()


def pick_kernel(n, picks_ref, parts_ref, out_ref):
    half = n // 2
    rows = out_ref.shape[1]
    block = rows // n
    part = parts_ref.shape[4]
    at = lax.broadcasted_iota(jnp.int32, (rows, rows), 0)
    u, rest = at // (2 * block), at % (2 * block)
    row = (rest // block) * (half * block) + u * block + rest % block
    hit = (picks_ref[...] == row).astype(jnp.float32).astype(jnp.bfloat16)
    for c in range(2):
        total = None
        for h in range(2):
            sides = [parts_ref[k, h * half : (h + 1) * half, c].reshape(rows, part) for k in range(2)]
            got = lax.dot_general(
                hit, jnp.concatenate(sides, axis=1), (((0,), (0,)), ((), ())), preferred_element_type=jnp.float32
            )
            total = got if total is None else total + got
        out_ref[c] = total


def solution(mesh):
    n = mesh.shape["stem"]

    def on_device(stem, edge_values, index_order, branch_first, branch_second, branch_third, edge_table, picks):
        _, _, rows, width = stem.shape
        open_width = branch_third.shape[2]
        part = open_width // 2
        block = rows // n
        chunk = rows // CHUNKS
        bf16, f32 = jnp.bfloat16, jnp.float32
        vmem = pl.BlockSpec(memory_space=pltpu.VMEM)
        anywhere = pl.BlockSpec(memory_space=pl.ANY)
        dma = pltpu.SemaphoreType.DMA
        parts = pl.pallas_call(
            functools.partial(contract_kernel, n),
            out_shape=jax.ShapeDtypeStruct((2, n, 2, 2 * block, part), bf16),
            in_specs=[pl.BlockSpec(memory_space=pltpu.HBM)] * 7,
            out_specs=anywhere,
            scratch_shapes=[
                pltpu.SMEM(edge_values.shape, edge_values.dtype),
                pltpu.VMEM((1, width), index_order.dtype),
                pltpu.VMEM(edge_table.shape, edge_table.dtype),
                pltpu.VMEM((2, rows, width), bf16),
                pltpu.VMEM((2, width, width), bf16),
                pltpu.VMEM((2, width, width), bf16),
                pltpu.VMEM((width, 2 * open_width), bf16),
                pltpu.VMEM((width // 2, width), bf16),
                pltpu.VMEM((width, 2 * open_width), bf16),
                pltpu.VMEM((width // 2, 2 * open_width), bf16),
                pltpu.VMEM((2 * chunk, width), bf16),
                pltpu.VMEM((CHUNKS, 4, chunk, open_width), f32),
                pltpu.VMEM((CHUNKS, 4, chunk, part), f32),
                pltpu.VMEM((n, 2, 2 * block, part), bf16),
                dma((7,)),
                dma((TILES,)),
                dma,
                dma((CHUNKS,)),
                dma((CHUNKS,)),
                dma((n,)),
                dma((n,)),
                dma((n,)),
                dma((n,)),
            ],
            compiler_params=pltpu.CompilerParams(
                collective_id=0, has_side_effects=True, vmem_limit_bytes=62 * 2**20
            ),
            cost_estimate=pl.CostEstimate(flops=8 * 10**9, bytes_accessed=13 * 2**20, transcendentals=0),
        )(
            edge_values, index_order.reshape(1, width), edge_table,
            stem[0], branch_first, branch_second, branch_third,
        )
        return pl.pallas_call(
            functools.partial(pick_kernel, n),
            out_shape=jax.ShapeDtypeStruct((2, picks.shape[0], open_width), f32),
            in_specs=[vmem, vmem],
            out_specs=vmem,
            compiler_params=pltpu.CompilerParams(vmem_limit_bytes=62 * 2**20),
        )(picks.reshape(1, picks.shape[0]), parts)

    return jax.shard_map(
        on_device,
        mesh=mesh,
        in_specs=(
            P(("groups", "cuts"), None, "stem", None),
            P(("groups", "cuts"), None),
            P(),
            P(),
            P(),
            P(),
            P(),
            P("stem"),
        ),
        out_specs=P(None, ("groups", "stem"), None),
        check_vma=False,
    )
```

```python
import functools

import jax
import jax.numpy as jnp
from jax import lax
from jax.experimental import pallas as pl
from jax.experimental.pallas import tpu as pltpu
from jax.sharding import PartitionSpec as P

MESH = pl.DeviceIdType.MESH
CHUNKS = 8
TILES = 4


def dot(a, b):
    return jnp.dot(a, b, preferred_element_type=jnp.float32)


def contract_kernel(
    n, edges_hbm, order_hbm, table_hbm, stem_hbm, first_hbm, second_hbm, third_hbm, out_hbm,
    edges_ref, order_ref, table_ref, stem, b1, b2, b3, pick, joint, gathered, firsts, partial, other, slab,
    load_sem, tile_sem, own_sem, pass_send, pass_recv, send_sem, recv_sem, copy_send, copy_recv,
):
    me = lax.axis_index("stem")
    core = lax.axis_index("cuts")
    mate = 1 - core
    half = n // 2
    top = me // half
    _, rows, width = stem.shape
    open_width = table_ref.shape[2]
    part = open_width // 2
    half_width = width // 2
    chunk = rows // CHUNKS
    block = rows // n
    owners = chunk // block

    tall = width // TILES
    loads = [
        pltpu.make_async_copy(third_hbm.at[0], b3.at[:, pl.ds(0, open_width)], load_sem.at[0]),
        pltpu.make_async_copy(third_hbm.at[1], b3.at[:, pl.ds(open_width, open_width)], load_sem.at[1]),
        pltpu.make_async_copy(order_hbm, order_ref, load_sem.at[2]),
        pltpu.make_async_copy(table_hbm, table_ref, load_sem.at[3]),
        pltpu.make_async_copy(edges_hbm, edges_ref, load_sem.at[4]),
    ]
    tiles = [
        pltpu.make_async_copy(
            second_hbm.at[:, pl.ds(at * tall, tall)], b2.at[:, pl.ds(at * tall, tall)], tile_sem.at[at]
        )
        for at in range(TILES)
    ]
    later = [
        pltpu.make_async_copy(stem_hbm, stem, load_sem.at[5]),
        pltpu.make_async_copy(first_hbm, b1, load_sem.at[6]),
    ]
    for load in loads + tiles:
        load.start()

    barrier = pltpu.get_barrier_semaphore()
    pl.semaphore_signal(barrier, inc=1, device_id={"cuts": mate}, device_id_type=MESH)

    @pl.loop(1, n)
    def _(step):
        pl.semaphore_signal(barrier, inc=1, device_id={"stem": (me + step) % n}, device_id_type=MESH)

    for load in loads:
        load.wait()
    wide = half_width // TILES
    for at in range(TILES):
        wanted = lax.broadcasted_iota(jnp.int32, (wide, width), 0) + (top * half_width + at * wide)
        hit = (order_ref[...] == wanted).astype(jnp.float32).astype(jnp.bfloat16)
        pick[at * wide : (at + 1) * wide, :] = hit

    code = edges_ref[0, 0]
    for edge in range(1, edges_ref.shape[1]):
        code = code + edges_ref[0, edge] * 2**edge
    factor = table_ref[code]
    factor_re, factor_im = factor[0:1], factor[1:2]

    for at in range(TILES):
        tiles[at].wait()
        if at == 0:
            for load in later:
                load.start()
        here = slice(at * tall, (at + 1) * tall)
        by_re = dot(b2[0, here, :], b3[...])
        by_im = dot(b2[1, here, :], b3[...])
        real = by_re[:, :open_width] - by_im[:, open_width:]
        imag = by_re[:, open_width:] + by_im[:, :open_width]
        joint[here, :open_width] = (real * factor_re - imag * factor_im).astype(jnp.bfloat16)
        joint[here, open_width:] = (real * factor_im + imag * factor_re).astype(jnp.bfloat16)

    gathered[...] = dot(pick[...], joint[...]).astype(jnp.bfloat16)

    for load in later:
        load.wait()

    def start_of(index):
        side = (1 - top + index // (CHUNKS // 2)) % 2
        count = CHUNKS // 2
        at = index % count
        return side * count + (at + (1 - me % 2) * (1 - 2 * (at % 2)))

    def passing(index):
        return pltpu.make_async_remote_copy(
            src_ref=partial.at[index, :, :, pl.ds(pl.multiple_of(mate * part, part), part)],
            dst_ref=other.at[index],
            send_sem=pass_send.at[index],
            recv_sem=pass_recv.at[index],
            device_id={"cuts": mate},
            device_id_type=MESH,
        )

    def sending(owner):
        return pltpu.make_async_remote_copy(
            src_ref=slab.at[owner],
            dst_ref=out_hbm.at[core, me],
            send_sem=send_sem.at[owner],
            recv_sem=recv_sem.at[me],
            device_id={"stem": owner},
            device_id_type=MESH,
        )

    def receiving(source):
        return pltpu.make_async_remote_copy(
            src_ref=slab.at[source],
            dst_ref=out_hbm.at[core, source],
            send_sem=send_sem.at[source],
            recv_sem=recv_sem.at[source],
            device_id={"stem": source},
            device_id_type=MESH,
        )

    def copying(source, src, column):
        return pltpu.make_async_remote_copy(
            src_ref=src,
            dst_ref=out_hbm.at[column, source],
            send_sem=copy_send.at[source],
            recv_sem=copy_recv.at[source],
            device_id={"cuts": mate},
            device_id_type=MESH,
        )

    def compute(index):
        here = pl.ds(pl.multiple_of(start_of(index) * chunk, chunk), chunk)
        step = open_width
        operand = stem[:, here, :].reshape(2 * chunk, width)
        for at in range(0, width, step):
            by_re = dot(operand, b1[0, :, at : at + step])
            by_im = dot(operand, b1[1, :, at : at + step])
            firsts[:chunk, at : at + step] = (by_re[:chunk] - by_im[chunk:]).astype(jnp.bfloat16)
            firsts[chunk:, at : at + step] = (by_im[:chunk] + by_re[chunk:]).astype(jnp.bfloat16)
        for t in range(2):
            got = dot(firsts[:, t * half_width : (t + 1) * half_width], gathered[...])
            partial[index, t] = got[:chunk, :open_width] - got[chunk:, open_width:]
            partial[index, 2 + t] = got[:chunk, open_width:] + got[chunk:, :open_width]

    def finish(last):
        passing(last).wait_recv()
        mine = pl.ds(pl.multiple_of(core * part, part), part)
        total = partial[last, :, :, mine] + other[last]
        for at in range(owners):
            owner = start_of(last) * owners + at
            for c in range(2):
                both = [total[2 * c + t, at * block : (at + 1) * block] for t in range(2)]
                slab[owner, c] = jnp.concatenate(both, axis=0).astype(jnp.bfloat16)

            @pl.when(owner != me)
            def _():
                sending(owner).start()

    compute(0)
    pl.semaphore_wait(barrier, n)
    passing(0).start()

    @pl.loop(1, CHUNKS)
    def _(index):
        compute(index)
        passing(index).start()
        finish(index - 1)

    finish(CHUNKS - 1)

    own = pltpu.make_async_copy(slab.at[me], out_hbm.at[core, me], own_sem)
    own.start()
    copying(me, slab.at[me], core).start()

    @pl.loop(1, n)
    def _(step):
        source = (me + step) % half + ((top + step // half) % 2) * half
        receiving(source).wait_recv()
        copying(source, out_hbm.at[core, source], core).start()

    own.wait()

    @pl.loop(0, n)
    def _(source):
        copying(source, out_hbm.at[core, source], mate).wait()

        @pl.when(source != me)
        def _():
            receiving(source).wait_send()

    @pl.loop(0, CHUNKS)
    def _(index):
        passing(index).wait_send()


def pick_kernel(n, picks_ref, parts_ref, out_ref):
    half = n // 2
    rows = out_ref.shape[1]
    block = rows // n
    part = parts_ref.shape[4]
    at = lax.broadcasted_iota(jnp.int32, (rows, rows), 0)
    u, rest = at // (2 * block), at % (2 * block)
    row = (rest // block) * (half * block) + u * block + rest % block
    hit = (picks_ref[...] == row).astype(jnp.float32).astype(jnp.bfloat16)
    for c in range(2):
        total = None
        for h in range(2):
            sides = [parts_ref[k, h * half : (h + 1) * half, c].reshape(rows, part) for k in range(2)]
            got = lax.dot_general(
                hit, jnp.concatenate(sides, axis=1), (((0,), (0,)), ((), ())), preferred_element_type=jnp.float32
            )
            total = got if total is None else total + got
        out_ref[c] = total


def solution(mesh):
    n = mesh.shape["stem"]

    def on_device(stem, edge_values, index_order, branch_first, branch_second, branch_third, edge_table, picks):
        _, _, rows, width = stem.shape
        open_width = branch_third.shape[2]
        part = open_width // 2
        block = rows // n
        chunk = rows // CHUNKS
        bf16, f32 = jnp.bfloat16, jnp.float32
        vmem = pl.BlockSpec(memory_space=pltpu.VMEM)
        anywhere = pl.BlockSpec(memory_space=pl.ANY)
        dma = pltpu.SemaphoreType.DMA
        parts = pl.pallas_call(
            functools.partial(contract_kernel, n),
            out_shape=jax.ShapeDtypeStruct((2, n, 2, 2 * block, part), bf16),
            in_specs=[pl.BlockSpec(memory_space=pltpu.HBM)] * 7,
            out_specs=anywhere,
            scratch_shapes=[
                pltpu.SMEM(edge_values.shape, edge_values.dtype),
                pltpu.VMEM((1, width), index_order.dtype),
                pltpu.VMEM(edge_table.shape, edge_table.dtype),
                pltpu.VMEM((2, rows, width), bf16),
                pltpu.VMEM((2, width, width), bf16),
                pltpu.VMEM((2, width, width), bf16),
                pltpu.VMEM((width, 2 * open_width), bf16),
                pltpu.VMEM((width // 2, width), bf16),
                pltpu.VMEM((width, 2 * open_width), bf16),
                pltpu.VMEM((width // 2, 2 * open_width), bf16),
                pltpu.VMEM((2 * chunk, width), bf16),
                pltpu.VMEM((CHUNKS, 4, chunk, open_width), f32),
                pltpu.VMEM((CHUNKS, 4, chunk, part), f32),
                pltpu.VMEM((n, 2, 2 * block, part), bf16),
                dma((7,)),
                dma((TILES,)),
                dma,
                dma((CHUNKS,)),
                dma((CHUNKS,)),
                dma((n,)),
                dma((n,)),
                dma((n,)),
                dma((n,)),
            ],
            compiler_params=pltpu.CompilerParams(
                collective_id=0, has_side_effects=True, vmem_limit_bytes=62 * 2**20
            ),
            cost_estimate=pl.CostEstimate(flops=8 * 10**9, bytes_accessed=13 * 2**20, transcendentals=0),
        )(
            edge_values, index_order.reshape(1, width), edge_table,
            stem[0], branch_first, branch_second, branch_third,
        )
        return pl.pallas_call(
            functools.partial(pick_kernel, n),
            out_shape=jax.ShapeDtypeStruct((2, picks.shape[0], open_width), f32),
            in_specs=[vmem, vmem],
            out_specs=vmem,
            compiler_params=pltpu.CompilerParams(vmem_limit_bytes=62 * 2**20),
        )(picks.reshape(1, picks.shape[0]), parts)

    return jax.shard_map(
        on_device,
        mesh=mesh,
        in_specs=(
            P(("groups", "cuts"), None, "stem", None),
            P(("groups", "cuts"), None),
            P(),
            P(),
            P(),
            P(),
            P(),
            P("stem"),
        ),
        out_specs=P(None, ("groups", "stem"), None),
        check_vma=False,
    )
```
